32 devices in a mesh: parts: 2 (over y), ship: 4 (over x, core), panel: 4 (over z).
Axes of the slice: x: 2, y: 2, z: 4, core: 2. Of those that a mesh axis runs over, the one named last changes fastest.
Arguments:
- right_side: float32 [8, 2, 32, 1024], P(('parts', 'ship'), None, None, 'panel'), parts along dimension 0, may hold values from -6 to 6
- current: bfloat16 [8, 2, 32, 1024], P(('parts', 'ship'), None, None, 'panel'), parts along dimension 0, may hold values from -6 to 6
- near_values: bfloat16 [8, 8, 6, 2, 128, 128], P(('parts', 'ship'), 'panel'), parts along dimension 0, may hold values from -0.15625 to 0.15625
- near_columns: int32 [8, 8, 6], P(('parts', 'ship'), 'panel'), parts along dimension 0, may hold values from 0 to 7, as said below
- block_inverse: bfloat16 [8, 8, 2, 128, 128], P(('parts', 'ship'), 'panel'), parts along dimension 0, may hold values from -1 to 2
- coupling_right: bfloat16 [8, 4, 2, 64, 1024], P('parts', 'ship', None, None, 'panel'), parts along dimension 0, may hold values from -0.125 to 0.125
- coupling_left: bfloat16 [8, 4, 2, 64, 1024], P(('parts', 'ship'), None, None, None, 'panel'), parts along dimension 0, may hold values from -0.26171875 to 0.26171875
- pair_rank: int32 [4, 4], replicated, may hold values from 32 to 64
- plan: int32 [3, 4], replicated, may hold values from 0 to 3, as said below
Outputs:
- field: float32 [8, 2, 32, 1024], P(('parts', 'ship'), None, None, 'panel'), parts along dimension 0
The draws below stay inside these ranges and needn't reach their ends.
There are 2 independent parts, one for each index of `parts`. The reference program is written for one: setup_inputs(seed, part) draws one part's arguments, and reference() takes and returns one part's arrays. A program takes and returns all parts, laid end to end along the dimension named above; an argument that names none is the same for every part. Nothing has to cross between parts.
Inputs may be any that keep to these rules, and one draw needn't show every extreme that they name: Each row is a pairing of the ships: plan[k, plan[k, s]] = s and plan[k, s] != s; every two ships are paired in exactly one round. `near_columns`: the entries of one block row are distinct and differ from the row's own block.
All inputs are finite; a program needn't handle non-finite values.
Results may differ from the reference program's by a relative error of at most 0.0046.
Values may be sent and summed in bfloat16 or wider, within the bound.
A program may use at most 64 MiB of HBM per device.

```python
import jax
import jax.numpy as jnp
from jax import lax

BLOCK = 128
RHS = 32
RANK = 64
NNZ = 6
SHIPS = 4
ROUNDS = 3
ROWS = 1024
NB = 8


def draw_near_columns(key, part):
    scores = jax.random.randint(key, (SHIPS, NB, NB - 1), 0, 1 << 20, dtype=jnp.int32)
    scores = scores * NB + lax.broadcasted_iota(jnp.int32, (SHIPS, NB, NB - 1), 2)
    chosen = lax.top_k(scores, NNZ)[1].astype(jnp.int32)
    row_ids = lax.broadcasted_iota(jnp.int32, (SHIPS, NB, NNZ), 1)
    return (row_ids + chosen + 1) % NB


def draw_block_inverse(key, part):
    shape = (SHIPS, NB, 2, BLOCK, BLOCK)
    eye_part = jnp.eye(BLOCK, dtype=jnp.float32)[None, None, None]
    real_only = (lax.broadcasted_iota(jnp.int32, shape, 2) == 0).astype(jnp.float32)
    noise = jnp.clip(jax.random.normal(key, shape, jnp.float32), -4.0, 4.0) * (0.25 / BLOCK ** 0.5)
    return (eye_part * real_only + noise).astype(jnp.bfloat16)


def draw_plan(key, part):
    first_key, second_key = jax.random.split(key)
    labels = jax.random.permutation(first_key, SHIPS).astype(jnp.int32)
    inverse = jnp.argsort(labels).astype(jnp.int32)
    order = jax.random.permutation(second_key, ROUNDS).astype(jnp.int32)
    last_label = SHIPS - 1
    round_ids = order[:, None]
    label_grid = labels[None, :]
    paired = jnp.where(label_grid == last_label, round_ids, jnp.where(label_grid == round_ids, last_label, (2 * round_ids - label_grid) % last_label))
    return inverse[paired].astype(jnp.int32)


def touch_ends(result, key, least, largest):
    dims = result.shape
    spot = [jax.random.randint(jax.random.fold_in(key, axis), (), 0, dims[axis]) for axis in range(len(dims))]
    result = result.at[tuple(spot)].set(least)
    longest = dims.index(max(dims))
    spot[longest] = (spot[longest] + 1) % dims[longest]
    return result.at[tuple(spot)].set(largest)


def level_of(rng, shape, cuts, smallest, largest):
    def one(dim, blocks):
        steps = jax.random.uniform(jax.random.fold_in(jax.random.fold_in(rng, 6), dim), (blocks,), jnp.float32, smallest / len(cuts), largest / len(cuts))
        return jnp.repeat(jnp.exp(steps), shape[dim] // blocks).reshape((-1,) + (1,) * (len(shape) - dim - 1))

    loudness = one(*cuts[0])
    for cut in cuts[1:]:
        loudness = loudness * one(*cut)
    return loudness


def centred(key, extent, scale, bound, shards=(), kind=jnp.bfloat16):
    values = jax.random.normal(key, extent, jnp.float32) * scale
    if len(shards) > 0:
        values = level_of(key, extent, shards, -0.22, 0.18) * values
    return jnp.clip(values, min=-bound, max=bound).astype(kind)


def setup_inputs(seed: int = 0, part: int = 0) -> dict:
    splits = jax.random.split(jax.random.key(seed), 10)
    part_keys = jax.random.split(jax.random.fold_in(splits[9], part), 10)
    right_side = centred(part_keys[0], (SHIPS, 2, RHS, ROWS), 1.0, 6.0, ((0, 4), (3, 4)), jnp.float32)
    current = centred(part_keys[1], (SHIPS, 2, RHS, ROWS), 1.0, 6.0, ((0, 4), (3, 4)))
    near_values = centred(part_keys[2], (SHIPS, NB, NNZ, 2, BLOCK, BLOCK), (2 * NNZ * BLOCK) ** -0.5, 0.15625, ((0, 4), (1, 4)))
    near_columns = draw_near_columns(jax.random.fold_in(jax.random.fold_in(splits[9], part), 71), part)
    block_inverse = draw_block_inverse(jax.random.fold_in(jax.random.fold_in(splits[9], part), 71), part)
    coupling_right = centred(part_keys[5], (SHIPS, SHIPS, 2, RANK, ROWS), (2 * ROWS) ** -0.5, 0.125, ((1, 4), (4, 4)))
    coupling_left = centred(part_keys[6], (SHIPS, SHIPS, 2, RANK, ROWS), (0.35 * RANK ** -0.5), 0.26171875, ((0, 4), (4, 4)))
    pair_rank = touch_ends(jax.random.randint(splits[7], (SHIPS, SHIPS), RANK // 2, RANK + 1), jax.random.fold_in(splits[7], 1), RANK // 2, RANK).astype(jnp.int32)
    plan = draw_plan(jax.random.fold_in(splits[9], 71), part)
    return dict(right_side=right_side, current=current, near_values=near_values, near_columns=near_columns, block_inverse=block_inverse, coupling_right=coupling_right, coupling_left=coupling_left, pair_rank=pair_rank, plan=plan)


def pair_up(product, rhs_count):
    real_src = product[:, :rhs_count]
    imag_src = product[:, rhs_count:]
    return jnp.stack([real_src[0] - imag_src[1], imag_src[0] + real_src[1]])


def near_field(values, columns, sources):
    rhs_count = sources.shape[1]
    block_len = values.shape[-1]
    cell_rows = sources.reshape(2 * rhs_count, -1, block_len)
    picked = jnp.take(cell_rows, columns.astype(jnp.int32), axis=1)
    product = jnp.einsum("cinu,inztu->zcit", picked.astype(jnp.float32), values.astype(jnp.float32))
    return pair_up(product, rhs_count).reshape(2, rhs_count, -1)


def apply_inverse(inverse, rest):
    rhs_count = rest.shape[1]
    block_len = inverse.shape[-1]
    rounded = rest.astype(jnp.bfloat16).reshape(2 * rhs_count, -1, block_len)
    product = jnp.einsum("ciu,iztu->zcit", rounded.astype(jnp.float32), inverse.astype(jnp.float32))
    return pair_up(product, rhs_count).reshape(2, rhs_count, -1)


def compress(right_basis, sent):
    rhs_count = sent.shape[1]
    flat = sent.reshape(2 * rhs_count, -1)
    grams = jnp.einsum("zan,cn->zac", right_basis.astype(jnp.float32), flat.astype(jnp.float32))
    return jnp.stack([grams[0, :, :rhs_count] - grams[1, :, rhs_count:], grams[0, :, rhs_count:] + grams[1, :, :rhs_count]])


def expand(received, left_basis):
    outer = jnp.einsum("yac,zan->yzcn", received.astype(jnp.float32), left_basis.astype(jnp.float32))
    return jnp.stack([outer[0, 0] - outer[1, 1], outer[0, 1] + outer[1, 0]])


def reference(right_side, current, near_values, near_columns, block_inverse, coupling_right, coupling_left, pair_rank, plan):
    def start_ship(operands):
        rhs_ship, current_ship, values_ship, columns_ship = operands
        return rhs_ship - near_field(values_ship, columns_ship, current_ship)

    rest = lax.map(start_ship, (right_side, current, near_values, near_columns))

    def invert_ship(operands):
        return apply_inverse(operands[0], operands[1])

    iterate = lax.map(invert_ship, (block_inverse, rest))
    rank_index = jnp.arange(RANK, dtype=jnp.int32)
    ship_index = jnp.arange(SHIPS, dtype=jnp.int32)
    for round_index in range(ROUNDS):
        partners = plan[round_index]
        sent = iterate.astype(jnp.bfloat16)

        def coupled_ship(ship):
            partner = partners[ship]
            grams = compress(coupling_right[ship, partner], sent[partner])
            keep_mask = rank_index < pair_rank[ship, partner]
            kept = jnp.where(keep_mask[None, :, None], grams, jnp.float32(0.0)).astype(jnp.bfloat16)
            return expand(kept, coupling_left[ship, partner])

        rest = rest - lax.map(coupled_ship, ship_index)
        iterate = lax.map(invert_ship, (block_inverse, rest))
    return iterate
```

```python
import functools
import itertools

import jax
import jax.numpy as jnp
from jax import lax
from jax.experimental import pallas as pl
from jax.experimental.pallas import tpu as pltpu
from jax.sharding import PartitionSpec as P

BF16 = jnp.bfloat16
F32 = jnp.float32


def dot_nt(a, b):
    return lax.dot_general(a, b, (((1,), (1,)), ((), ())), preferred_element_type=F32)


def dot_nn(a, b):
    return lax.dot_general(a, b, (((1,), (0,)), ((), ())), preferred_element_type=F32)


def partner_of(ship, match):
    if match == 1:
        return ship + 1 - 2 * (ship % 2)
    if match == 2:
        return ship + 2 - 4 * (ship // 2)
    return 3 - ship


def complex_pair(product, rows, cols):
    real = product[:rows, :cols] - product[rows:, cols:]
    imag = product[rows:, :cols] + product[:rows, cols:]
    return real, imag


def sweep_kernel(
    order,
    panels,
    near_columns,
    pair_rank,
    right_side,
    current,
    near_values,
    block_inverse,
    coupling_right,
    coupling_left,
    field,
    ring,
    side,
    values,
    inverse,
    right,
    left,
    outbox,
    slots,
    load_sem,
    gather_send,
    gather_recv,
    round_send,
    round_recv,
):
    ship = lax.axis_index("ship")
    panel = lax.axis_index("panel")
    blocks, terms = near_values.shape[1], near_values.shape[2]
    block = near_values.shape[-1]
    rhs = current.shape[2]
    rank = coupling_left.shape[3]
    rounds = len(order)
    partners = [partner_of(ship, match) for match in order]

    barrier = pltpu.get_barrier_semaphore()
    for step in range(1, panels):
        pl.semaphore_signal(
            barrier,
            inc=1,
            device_id={"panel": (panel + step) % panels},
            device_id_type=pl.DeviceIdType.MESH,
        )
    for partner in partners:
        for target in range(panels):
            pl.semaphore_signal(
                barrier,
                inc=1,
                device_id={"ship": partner, "panel": target},
                device_id_type=pl.DeviceIdType.MESH,
            )

    own = [
        pltpu.make_async_copy(
            current.at[0, :, :, b * block : (b + 1) * block],
            ring.at[panel * blocks + b],
            load_sem.at[b],
        )
        for b in range(blocks)
    ]
    bases = [
        pltpu.make_async_copy(block_inverse.at[0], inverse, load_sem.at[blocks]),
        pltpu.make_async_copy(coupling_left.at[0], left, load_sem.at[blocks + 1]),
        pltpu.make_async_copy(coupling_right, right, load_sem.at[blocks + 2]),
    ]
    near_loads = [
        pltpu.make_async_copy(right_side.at[0], side, load_sem.at[blocks + 3]),
        pltpu.make_async_copy(near_values.at[0], values, load_sem.at[blocks + 4]),
    ]
    for copy in own + bases + near_loads:
        copy.start()
    for copy in own:
        copy.wait()

    pl.semaphore_wait(barrier, panels - 1 + rounds * panels)
    mine = ring.at[pl.ds(panel * blocks, blocks)]
    spread = [
        pltpu.make_async_remote_copy(
            src_ref=mine,
            dst_ref=mine,
            send_sem=gather_send.at[step - 1],
            recv_sem=gather_recv.at[step - 1],
            device_id={"panel": (panel + step) % panels},
            device_id_type=pl.DeviceIdType.MESH,
        )
        for step in range(1, panels)
    ]
    for copy in spread:
        copy.start()

    for copy in bases:
        copy.wait()
    inv = [inverse[b].reshape(2 * block, block) for b in range(blocks)]
    raw = [left[p] for p in partners]
    moved = []
    for b in range(blocks):
        rows = jnp.concatenate(
            [r[y, :, b * block : (b + 1) * block] for y in range(2) for r in raw], axis=0
        )
        moved.append(complex_pair(dot_nt(rows, inv[b]), rounds * rank, block))
    moved_re = jnp.concatenate([m[0] for m in moved], axis=1)
    moved_im = jnp.concatenate([m[1] for m in moved], axis=1)
    spreaders = []
    for k in range(rounds):
        re, im = moved_re[k * rank : (k + 1) * rank], moved_im[k * rank : (k + 1) * rank]
        spreaders.append(
            jnp.concatenate(
                [jnp.concatenate([re, im], axis=1), jnp.concatenate([-im, re], axis=1)], axis=0
            ).astype(BF16)
        )
    gatherers = []
    for p in partners:
        re, im = right[p, 0, 0], right[p, 0, 1]
        gatherers.append(
            jnp.concatenate(
                [jnp.concatenate([re, -im], axis=1), jnp.concatenate([im, re], axis=1)], axis=0
            )
        )
    links = {
        (k, j): dot_nt(spreaders[j], gatherers[k]).astype(BF16)
        for k in range(rounds)
        for j in range(k)
    }

    for copy in near_loads:
        copy.wait()
    for copy in spread:
        copy.wait_recv()

    start_re, start_im = [], []
    for b in range(blocks):
        picked = jnp.concatenate(
            [ring[near_columns[0, b, n]].reshape(2 * rhs, block) for n in range(terms)], axis=1
        )
        weights = jnp.concatenate(
            [values[b, n].reshape(2 * block, block) for n in range(terms)], axis=1
        )
        re, im = complex_pair(dot_nt(picked, weights), rhs, block)
        cols = slice(b * block, (b + 1) * block)
        rest = jnp.concatenate([side[0, :, cols] - re, side[1, :, cols] - im], axis=0)
        re, im = complex_pair(dot_nt(rest.astype(BF16), inv[b]), rhs, block)
        start_re.append(re)
        start_im.append(im)
    total = jnp.concatenate(start_re + start_im, axis=1)
    sent = total.astype(BF16)
    parts = [dot_nt(sent, g) for g in gatherers]

    lane = lax.broadcasted_iota(jnp.int32, (rhs, 2 * rank), 1)
    lane = jnp.where(lane < rank, lane, lane - rank)
    flights = []
    for k in range(rounds):
        outbox[k] = parts[k].astype(BF16)
        copies = [
            pltpu.make_async_remote_copy(
                src_ref=outbox.at[k],
                dst_ref=slots.at[k, step],
                send_sem=round_send.at[k, step],
                recv_sem=round_recv.at[k, step],
                device_id={"ship": partners[k], "panel": (panel + step) % panels},
                device_id_type=pl.DeviceIdType.MESH,
            )
            for step in range(panels)
        ]
        for copy in copies:
            copy.start()
        flights += copies
        if k > 0:
            total = total - dot_nn(received, spreaders[k - 1])
            for later in range(k + 1, rounds):
                parts[later] = parts[later] - dot_nn(received, links[later, k - 1])
        for copy in copies:
            copy.wait_recv()
        summed = slots[k, 0].astype(F32)
        for source in range(1, panels):
            summed = summed + slots[k, source].astype(F32)
        kept = pair_rank[ship, partners[k]]
        received = jnp.where(lane < kept, summed, 0.0).astype(BF16)
        if k + 1 < rounds:
            parts[k + 1] = parts[k + 1] - dot_nn(received, links[k + 1, k])
    total = total - dot_nn(received, spreaders[rounds - 1])
    width = blocks * block
    field[0, 0] = total[:, :width]
    field[0, 1] = total[:, width:]
    for copy in spread + flights:
        copy.wait_send()


def sweep_call(order, collective_id, panels, operands):
    (right_side, current, near_values, near_columns, block_inverse, coupling_right, coupling_left, pair_rank) = operands
    blocks = near_values.shape[1]
    block = near_values.shape[-1]
    rhs = current.shape[2]
    rank = coupling_left.shape[3]
    rounds = len(order)
    anywhere = pl.BlockSpec(memory_space=pl.ANY)
    scalars = pl.BlockSpec(memory_space=pltpu.SMEM)
    return pl.pallas_call(
        functools.partial(sweep_kernel, order, panels),
        out_shape=jax.ShapeDtypeStruct(right_side.shape, F32),
        in_specs=[scalars, scalars] + [anywhere] * 6,
        out_specs=pl.BlockSpec(memory_space=pltpu.VMEM),
        scratch_shapes=[
            pltpu.VMEM((panels * blocks, 2, rhs, block), BF16),
            pltpu.VMEM(right_side.shape[1:], F32),
            pltpu.VMEM(near_values.shape[1:], BF16),
            pltpu.VMEM(block_inverse.shape[1:], BF16),
            pltpu.VMEM(coupling_right.shape, BF16),
            pltpu.VMEM(coupling_left.shape[1:], BF16),
            pltpu.VMEM((rounds, rhs, 2 * rank), BF16),
            pltpu.VMEM((rounds, panels, rhs, 2 * rank), BF16),
            pltpu.SemaphoreType.DMA((blocks + 5,)),
            pltpu.SemaphoreType.DMA((panels - 1,)),
            pltpu.SemaphoreType.DMA((panels - 1,)),
            pltpu.SemaphoreType.DMA((rounds, panels)),
            pltpu.SemaphoreType.DMA((rounds, panels)),
        ],
        compiler_params=pltpu.CompilerParams(
            collective_id=collective_id,
            has_side_effects=True,
            vmem_limit_bytes=24 * 1024 * 1024,
        ),
    )(
        near_columns,
        pair_rank,
        right_side,
        current,
        near_values,
        block_inverse,
        coupling_right,
        coupling_left,
    )


def four_ships(panels, right_side, current, near_values, near_columns, block_inverse, coupling_right, coupling_left, pair_rank, plan):
    orders = list(itertools.permutations((1, 2, 3)))
    index = 2 * (plan[0, 0] - 1) + (plan[1, 0] > plan[2, 0]).astype(jnp.int32)
    operands = (right_side, current, near_values, near_columns, block_inverse, coupling_right, coupling_left, pair_rank)
    branches = [
        functools.partial(lambda order, number, *args: sweep_call(order, number, panels, args), order, number)
        for number, order in enumerate(orders)
    ]
    return lax.switch(index, branches, *operands)


def pair_up(product, rhs_count):
    real_src = product[:, :rhs_count]
    imag_src = product[:, rhs_count:]
    return jnp.stack([real_src[0] - imag_src[1], imag_src[0] + real_src[1]])


def near_field(values, columns, gathered):
    rhs_count = gathered.shape[1]
    block_len = values.shape[-1]
    cell_rows = gathered.reshape(2 * rhs_count, -1, block_len)
    picked = jnp.stack(
        [
            jnp.stack(
                [
                    lax.dynamic_index_in_dim(cell_rows, columns[i, n], 1, keepdims=False)
                    for n in range(columns.shape[1])
                ],
                axis=1,
            )
            for i in range(columns.shape[0])
        ],
        axis=1,
    )
    product = jnp.einsum("cinu,inztu->zcit", picked, values, preferred_element_type=jnp.float32)
    return pair_up(product, rhs_count).reshape(2, rhs_count, -1)


def apply_inverse(inverse, rest):
    rhs_count = rest.shape[1]
    block_len = inverse.shape[-1]
    rounded = rest.astype(jnp.bfloat16).reshape(2 * rhs_count, -1, block_len)
    product = jnp.einsum("ciu,iztu->zcit", rounded, inverse, preferred_element_type=jnp.float32)
    return pair_up(product, rhs_count).reshape(2, rhs_count, -1)


def compress(right_basis, sent):
    rhs_count = sent.shape[1]
    flat = sent.reshape(2 * rhs_count, -1)
    grams = jnp.einsum("zan,cn->zac", right_basis, flat, preferred_element_type=jnp.float32)
    return jnp.stack(
        [
            grams[0, :, :rhs_count] - grams[1, :, rhs_count:],
            grams[0, :, rhs_count:] + grams[1, :, :rhs_count],
        ]
    )


def expand(received, left_basis):
    outer = jnp.einsum("yac,zan->yzcn", received, left_basis, preferred_element_type=jnp.float32)
    return jnp.stack([outer[0, 0] - outer[1, 1], outer[0, 1] + outer[1, 0]])


def any_ships(
    right_side,
    current,
    near_values,
    near_columns,
    block_inverse,
    coupling_right,
    coupling_left,
    pair_rank,
    plan,
):
    gathered = lax.all_gather(current[0], "panel", axis=2, tiled=True)
    rest = right_side[0] - near_field(near_values[0], near_columns[0], gathered)
    iterate = apply_inverse(block_inverse[0], rest)
    own_ship = lax.axis_index("ship")
    ship_count = coupling_left.shape[1]
    rank_index = lax.iota(jnp.int32, coupling_left.shape[3])
    for round_index in range(plan.shape[0]):
        partner = plan[round_index, own_ship]
        right_basis = lax.dynamic_index_in_dim(coupling_right, partner, 0, keepdims=False)[0]
        partial_value = compress(right_basis, iterate.astype(jnp.bfloat16))
        slot_mask = (lax.iota(jnp.int32, ship_count) == partner).astype(jnp.float32)
        spread = slot_mask[:, None, None, None] * partial_value[None]
        summed = lax.psum(spread, ("ship", "panel"))
        incoming = lax.dynamic_index_in_dim(summed, own_ship, 0, keepdims=False)
        keep_mask = rank_index < pair_rank[own_ship, partner]
        received = jnp.where(keep_mask[None, :, None], incoming, jnp.float32(0.0)).astype(
            jnp.bfloat16
        )
        left_basis = lax.dynamic_index_in_dim(coupling_left[0], partner, 0, keepdims=False)
        rest = rest - expand(received, left_basis)
        iterate = apply_inverse(block_inverse[0], rest)
    return iterate[None]


def solution(mesh):
    placed = (
        P(("parts", "ship"), None, None, "panel"),
        P(("parts", "ship"), None, None, "panel"),
        P(("parts", "ship"), "panel", None, None, None, None),
        P(("parts", "ship"), "panel", None),
        P(("parts", "ship"), "panel", None, None, None),
        P("parts", "ship", None, None, "panel"),
        P(("parts", "ship"), None, None, None, "panel"),
        P(),
        P(),
    )
    ships, panels = mesh.shape["ship"], mesh.shape["panel"]
    on_device = functools.partial(four_ships, panels) if ships == 4 and panels <= 8 else any_ships
    return jax.shard_map(
        on_device,
        mesh=mesh,
        in_specs=placed,
        out_specs=P(("parts", "ship"), None, None, "panel"),
        check_vma=False,
    )
```

```python
import functools

import jax
import jax.numpy as jnp
from jax import lax
from jax.experimental import pallas as pl
from jax.experimental.pallas import tpu as pltpu
from jax.sharding import PartitionSpec as P

BF16 = jnp.bfloat16
F32 = jnp.float32


def dot_nt(a, b):
    return lax.dot_general(a, b, (((1,), (1,)), ((), ())), preferred_element_type=F32)


def dot_nn(a, b):
    return lax.dot_general(a, b, (((1,), (0,)), ((), ())), preferred_element_type=F32)


def complex_pair(product, rows, cols):
    real = product[:rows, :cols] - product[rows:, cols:]
    imag = product[rows:, :cols] + product[:rows, cols:]
    return real, imag


def times_i(real, imag):
    return jnp.concatenate(
        [jnp.concatenate([real, imag], axis=1), jnp.concatenate([-imag, real], axis=1)], axis=0
    )


def sweep_kernel(
    ships,
    panels,
    columns_hbm,
    rank_hbm,
    plan_hbm,
    right_side,
    current,
    near_values,
    block_inverse,
    coupling_right,
    coupling_left,
    field,
    near_columns,
    pair_rank,
    plan,
    ring,
    side,
    values,
    inverse,
    right,
    left,
    link_out,
    link_in,
    all_links,
    part_out,
    part_in,
    all_parts,
    load_sem,
    panel_send,
    panel_recv,
    ship_send,
    ship_recv,
):
    ship = lax.axis_index("ship")
    panel = lax.axis_index("panel")
    blocks, terms = near_values.shape[1], near_values.shape[2]
    block = near_values.shape[-1]
    rhs = current.shape[2]
    rank = coupling_left.shape[3]
    rounds = plan.shape[0]
    pairs = [(k, j) for k in range(rounds) for j in range(k)]

    def to_panels(stage, source, target):
        return [
            pltpu.make_async_remote_copy(
                src_ref=source(step),
                dst_ref=target(step),
                send_sem=panel_send.at[stage, step - 1],
                recv_sem=panel_recv.at[stage, step - 1],
                device_id={"panel": (panel + step) % panels},
                device_id_type=pl.DeviceIdType.MESH,
            )
            for step in range(1, panels)
        ]

    def to_ships(stage, ref):
        return [
            pltpu.make_async_remote_copy(
                src_ref=ref,
                dst_ref=ref,
                send_sem=ship_send.at[stage, step - 1],
                recv_sem=ship_recv.at[stage, step - 1],
                device_id={"ship": (ship + step) % ships},
                device_id_type=pl.DeviceIdType.MESH,
            )
            for step in range(1, ships)
        ]

    barrier = pltpu.get_barrier_semaphore()
    for step in range(1, panels):
        pl.semaphore_signal(
            barrier,
            inc=1,
            device_id={"panel": (panel + step) % panels},
            device_id_type=pl.DeviceIdType.MESH,
        )
    for step in range(1, ships):
        pl.semaphore_signal(
            barrier,
            inc=1,
            device_id={"ship": (ship + step) % ships},
            device_id_type=pl.DeviceIdType.MESH,
        )

    own = [
        pltpu.make_async_copy(
            current.at[0, :, :, b * block : (b + 1) * block],
            ring.at[panel * blocks + b],
            load_sem.at[b],
        )
        for b in range(blocks)
    ]
    bases = [
        pltpu.make_async_copy(plan_hbm, plan, load_sem.at[blocks]),
        pltpu.make_async_copy(block_inverse.at[0], inverse, load_sem.at[blocks + 1]),
        pltpu.make_async_copy(coupling_left.at[0], left, load_sem.at[blocks + 2]),
        pltpu.make_async_copy(coupling_right, right, load_sem.at[blocks + 3]),
    ]
    near_loads = [
        pltpu.make_async_copy(columns_hbm, near_columns, load_sem.at[blocks + 4]),
        pltpu.make_async_copy(rank_hbm, pair_rank, load_sem.at[blocks + 5]),
        pltpu.make_async_copy(right_side.at[0], side, load_sem.at[blocks + 6]),
        pltpu.make_async_copy(near_values.at[0], values, load_sem.at[blocks + 7]),
    ]
    for copy in own + bases + near_loads:
        copy.start()
    for copy in own:
        copy.wait()

    pl.semaphore_wait(barrier, panels - 1 + ships - 1)
    mine = ring.at[pl.ds(panel * blocks, blocks)]
    spread = to_panels(0, lambda step: mine, lambda step: mine)
    for copy in spread:
        copy.start()

    for copy in bases:
        copy.wait()
    partners = [plan[k, ship] for k in range(rounds)]
    inv = [inverse[b].reshape(2 * block, block) for b in range(blocks)]
    raw = [left[p] for p in partners]
    moved = []
    for b in range(blocks):
        rows = jnp.concatenate(
            [r[y, :, b * block : (b + 1) * block] for y in range(2) for r in raw], axis=0
        )
        moved.append(complex_pair(dot_nt(rows, inv[b]), rounds * rank, block))
    moved_re = jnp.concatenate([m[0] for m in moved], axis=1)
    moved_im = jnp.concatenate([m[1] for m in moved], axis=1)
    spreaders = []
    for k in range(rounds):
        cut = slice(k * rank, (k + 1) * rank)
        spreaders.append(times_i(moved_re[cut], moved_im[cut]).astype(BF16))
    gatherers = []
    for p in partners:
        re, im = right[p, 0, 0], right[p, 0, 1]
        gatherers.append(
            jnp.concatenate(
                [jnp.concatenate([re, -im], axis=1), jnp.concatenate([im, re], axis=1)], axis=0
            )
        )
    share = rank // panels
    for index, (k, j) in enumerate(pairs):
        link = dot_nt(spreaders[j][:rank], gatherers[k]).astype(BF16)
        for target in range(panels):
            link_out[target, index] = link[target * share : (target + 1) * share]
    scatter = to_panels(
        1, lambda step: link_out.at[(panel + step) % panels], lambda step: link_in.at[step - 1]
    )
    for copy in scatter:
        copy.start()

    for copy in near_loads:
        copy.wait()
    for copy in spread:
        copy.wait_recv()

    start_re, start_im = [], []
    for b in range(blocks):
        picked = jnp.concatenate(
            [ring[near_columns[0, b, n]].reshape(2 * rhs, block) for n in range(terms)], axis=1
        )
        weights = jnp.concatenate(
            [values[b, n].reshape(2 * block, block) for n in range(terms)], axis=1
        )
        re, im = complex_pair(dot_nt(picked, weights), rhs, block)
        cols = slice(b * block, (b + 1) * block)
        rest = jnp.concatenate([side[0, :, cols] - re, side[1, :, cols] - im], axis=0)
        re, im = complex_pair(dot_nt(rest.astype(BF16), inv[b]), rhs, block)
        start_re.append(re)
        start_im.append(im)
    total = jnp.concatenate(start_re + start_im, axis=1)
    sent = total.astype(BF16)
    own_parts = [dot_nt(sent, g) for g in gatherers]
    for k in range(rounds):
        part_out[k] = own_parts[k].astype(BF16)
    part_flight = to_panels(2, lambda step: part_out, lambda step: part_in.at[step - 1])
    for copy in part_flight:
        copy.start()

    for copy in scatter:
        copy.wait_recv()
    for index in range(len(pairs)):
        summed = link_out[panel, index].astype(F32)
        for step in range(1, panels):
            summed = summed + link_in[step - 1, index].astype(F32)
        all_links[ship, panel, index] = summed.astype(BF16)
    piece = all_links.at[ship, panel]
    link_flight = to_panels(3, lambda step: piece, lambda step: piece)
    for copy in link_flight:
        copy.start()

    for copy in part_flight:
        copy.wait_recv()
    for k in range(rounds):
        summed = own_parts[k]
        for step in range(1, panels):
            summed = summed + part_in[step - 1, k].astype(F32)
        all_parts[ship, k] = summed.astype(BF16)
    part_ships = to_ships(0, all_parts.at[ship])
    for copy in part_ships:
        copy.start()
    for copy in link_flight:
        copy.wait_recv()
    link_ships = to_ships(1, all_links.at[ship])
    for copy in link_ships:
        copy.start()
    for copy in part_ships + link_ships:
        copy.wait_recv()

    lane = lax.broadcasted_iota(jnp.int32, (rhs, 2 * rank), 1)
    lane = jnp.where(lane < rank, lane, lane - rank)

    def received(k, target, partner):
        value = all_parts[partner, k].astype(F32)
        for j in range(k):
            index = pairs.index((k, j))
            rows = jnp.concatenate(
                [all_links[partner, q, index] for q in range(panels)], axis=0
            ).astype(F32)
            link = times_i(rows[:, :rank], rows[:, rank:]).astype(BF16)
            value = value - dot_nn(received(j, partner, plan[j, partner]), link)
        return jnp.where(lane < pair_rank[target, partner], value, 0.0).astype(BF16)

    for k in range(rounds):
        total = total - dot_nn(received(k, ship, partners[k]), spreaders[k])
    width = blocks * block
    field[0, 0] = total[:, :width]
    field[0, 1] = total[:, width:]
    for copy in spread + scatter + part_flight + link_flight + part_ships + link_ships:
        copy.wait_send()


def few_ships(ships, panels, right_side, current, near_values, near_columns, block_inverse, coupling_right, coupling_left, pair_rank, plan):
    blocks = near_values.shape[1]
    block = near_values.shape[-1]
    rhs = current.shape[2]
    rank = coupling_left.shape[3]
    rounds = plan.shape[0]
    links = rounds * (rounds - 1) // 2
    share = rank // panels
    anywhere = pl.BlockSpec(memory_space=pl.ANY)
    return pl.pallas_call(
        functools.partial(sweep_kernel, ships, panels),
        out_shape=jax.ShapeDtypeStruct(right_side.shape, F32),
        in_specs=[anywhere] * 9,
        out_specs=pl.BlockSpec(memory_space=pltpu.VMEM),
        scratch_shapes=[
            pltpu.SMEM(near_columns.shape, jnp.int32),
            pltpu.SMEM(pair_rank.shape, jnp.int32),
            pltpu.SMEM(plan.shape, jnp.int32),
            pltpu.VMEM((panels * blocks, 2, rhs, block), BF16),
            pltpu.VMEM(right_side.shape[1:], F32),
            pltpu.VMEM(near_values.shape[1:], BF16),
            pltpu.VMEM(block_inverse.shape[1:], BF16),
            pltpu.VMEM(coupling_right.shape, BF16),
            pltpu.VMEM(coupling_left.shape[1:], BF16),
            pltpu.VMEM((panels, links, share, 2 * rank), BF16),
            pltpu.VMEM((panels - 1, links, share, 2 * rank), BF16),
            pltpu.VMEM((ships, panels, links, share, 2 * rank), BF16),
            pltpu.VMEM((rounds, rhs, 2 * rank), BF16),
            pltpu.VMEM((panels - 1, rounds, rhs, 2 * rank), BF16),
            pltpu.VMEM((ships, rounds, rhs, 2 * rank), BF16),
            pltpu.SemaphoreType.DMA((blocks + 8,)),
            pltpu.SemaphoreType.DMA((4, panels - 1)),
            pltpu.SemaphoreType.DMA((4, panels - 1)),
            pltpu.SemaphoreType.DMA((2, ships - 1)),
            pltpu.SemaphoreType.DMA((2, ships - 1)),
        ],
        compiler_params=pltpu.CompilerParams(
            collective_id=0,
            has_side_effects=True,
            vmem_limit_bytes=60 * 1024 * 1024,
        ),
    )(
        near_columns,
        pair_rank,
        plan,
        right_side,
        current,
        near_values,
        block_inverse,
        coupling_right,
        coupling_left,
    )


def pair_up(product, rhs_count):
    real_src = product[:, :rhs_count]
    imag_src = product[:, rhs_count:]
    return jnp.stack([real_src[0] - imag_src[1], imag_src[0] + real_src[1]])


def near_field(values, columns, gathered):
    rhs_count = gathered.shape[1]
    block_len = values.shape[-1]
    cell_rows = gathered.reshape(2 * rhs_count, -1, block_len)
    picked = jnp.stack(
        [
            jnp.stack(
                [
                    lax.dynamic_index_in_dim(cell_rows, columns[i, n], 1, keepdims=False)
                    for n in range(columns.shape[1])
                ],
                axis=1,
            )
            for i in range(columns.shape[0])
        ],
        axis=1,
    )
    product = jnp.einsum("cinu,inztu->zcit", picked, values, preferred_element_type=jnp.float32)
    return pair_up(product, rhs_count).reshape(2, rhs_count, -1)


def apply_inverse(inverse, rest):
    rhs_count = rest.shape[1]
    block_len = inverse.shape[-1]
    rounded = rest.astype(jnp.bfloat16).reshape(2 * rhs_count, -1, block_len)
    product = jnp.einsum("ciu,iztu->zcit", rounded, inverse, preferred_element_type=jnp.float32)
    return pair_up(product, rhs_count).reshape(2, rhs_count, -1)


def compress(right_basis, sent):
    rhs_count = sent.shape[1]
    flat = sent.reshape(2 * rhs_count, -1)
    grams = jnp.einsum("zan,cn->zac", right_basis, flat, preferred_element_type=jnp.float32)
    return jnp.stack(
        [
            grams[0, :, :rhs_count] - grams[1, :, rhs_count:],
            grams[0, :, rhs_count:] + grams[1, :, :rhs_count],
        ]
    )


def expand(received, left_basis):
    outer = jnp.einsum("yac,zan->yzcn", received, left_basis, preferred_element_type=jnp.float32)
    return jnp.stack([outer[0, 0] - outer[1, 1], outer[0, 1] + outer[1, 0]])


def any_ships(
    right_side,
    current,
    near_values,
    near_columns,
    block_inverse,
    coupling_right,
    coupling_left,
    pair_rank,
    plan,
):
    gathered = lax.all_gather(current[0], "panel", axis=2, tiled=True)
    rest = right_side[0] - near_field(near_values[0], near_columns[0], gathered)
    iterate = apply_inverse(block_inverse[0], rest)
    own_ship = lax.axis_index("ship")
    ship_count = coupling_left.shape[1]
    rank_index = lax.iota(jnp.int32, coupling_left.shape[3])
    for round_index in range(plan.shape[0]):
        partner = plan[round_index, own_ship]
        right_basis = lax.dynamic_index_in_dim(coupling_right, partner, 0, keepdims=False)[0]
        partial_value = compress(right_basis, iterate.astype(jnp.bfloat16))
        slot_mask = (lax.iota(jnp.int32, ship_count) == partner).astype(jnp.float32)
        spread = slot_mask[:, None, None, None] * partial_value[None]
        summed = lax.psum(spread, ("ship", "panel"))
        incoming = lax.dynamic_index_in_dim(summed, own_ship, 0, keepdims=False)
        keep_mask = rank_index < pair_rank[own_ship, partner]
        received = jnp.where(keep_mask[None, :, None], incoming, jnp.float32(0.0)).astype(
            jnp.bfloat16
        )
        left_basis = lax.dynamic_index_in_dim(coupling_left[0], partner, 0, keepdims=False)
        rest = rest - expand(received, left_basis)
        iterate = apply_inverse(block_inverse[0], rest)
    return iterate[None]


def solution(mesh):
    placed = (
        P(("parts", "ship"), None, None, "panel"),
        P(("parts", "ship"), None, None, "panel"),
        P(("parts", "ship"), "panel", None, None, None, None),
        P(("parts", "ship"), "panel", None),
        P(("parts", "ship"), "panel", None, None, None),
        P("parts", "ship", None, None, "panel"),
        P(("parts", "ship"), None, None, None, "panel"),
        P(),
        P(),
    )
    ships, panels = mesh.shape["ship"], mesh.shape["panel"]
    on_device = functools.partial(few_ships, ships, panels) if ships == 4 and panels == 4 else any_ships
    return jax.shard_map(
        on_device,
        mesh=mesh,
        in_specs=placed,
        out_specs=P(("parts", "ship"), None, None, "panel"),
        check_vma=False,
    )
```

```python
import functools

import jax
import jax.numpy as jnp
from jax import lax
from jax.experimental import pallas as pl
from jax.experimental.pallas import tpu as pltpu
from jax.sharding import PartitionSpec as P

BF16 = jnp.bfloat16
F32 = jnp.float32


def dot_nt(a, b):
    return lax.dot_general(a, b, (((1,), (1,)), ((), ())), preferred_element_type=F32)


def dot_nn(a, b):
    return lax.dot_general(a, b, (((1,), (0,)), ((), ())), preferred_element_type=F32)


def complex_pair(product, rows, cols):
    real = product[:rows, :cols] - product[rows:, cols:]
    imag = product[rows:, :cols] + product[:rows, cols:]
    return real, imag


def times_i(real, imag):
    return jnp.concatenate(
        [jnp.concatenate([real, imag], axis=1), jnp.concatenate([-imag, real], axis=1)], axis=0
    )


def sweep_kernel(
    ships,
    panels,
    columns_hbm,
    rank_hbm,
    plan_hbm,
    right_side,
    current,
    near_values,
    block_inverse,
    coupling_right,
    coupling_left,
    field,
    near_columns,
    pair_rank,
    plan,
    ring,
    side,
    values,
    inverse,
    right,
    left,
    link_out,
    link_in,
    all_links,
    part_out,
    part_in,
    all_parts,
    load_sem,
    panel_send,
    panel_recv,
    ship_send,
    ship_recv,
):
    ship = lax.axis_index("ship")
    panel = lax.axis_index("panel")
    blocks, terms = near_values.shape[1], near_values.shape[2]
    block = near_values.shape[-1]
    rhs = current.shape[2]
    rank = coupling_left.shape[3]
    rounds = plan.shape[0]
    pairs = [(k, j) for k in range(rounds) for j in range(k)]

    def to_panels(stage, source, target):
        return [
            pltpu.make_async_remote_copy(
                src_ref=source(step),
                dst_ref=target(step),
                send_sem=panel_send.at[stage, step - 1],
                recv_sem=panel_recv.at[stage, step - 1],
                device_id={"panel": (panel + step) % panels},
                device_id_type=pl.DeviceIdType.MESH,
            )
            for step in range(1, panels)
        ]

    def to_ships(stage, ref):
        return [
            pltpu.make_async_remote_copy(
                src_ref=ref,
                dst_ref=ref,
                send_sem=ship_send.at[stage, step - 1],
                recv_sem=ship_recv.at[stage, step - 1],
                device_id={"ship": (ship + step) % ships},
                device_id_type=pl.DeviceIdType.MESH,
            )
            for step in range(1, ships)
        ]

    barrier = pltpu.get_barrier_semaphore()
    for step in range(1, panels):
        pl.semaphore_signal(
            barrier,
            inc=1,
            device_id={"panel": (panel + step) % panels},
            device_id_type=pl.DeviceIdType.MESH,
        )
    for step in range(1, ships):
        pl.semaphore_signal(
            barrier,
            inc=1,
            device_id={"ship": (ship + step) % ships},
            device_id_type=pl.DeviceIdType.MESH,
        )

    own = pltpu.make_async_copy(current.at[0], ring.at[panel], load_sem.at[8])
    bases = [
        pltpu.make_async_copy(plan_hbm, plan, load_sem.at[0]),
        pltpu.make_async_copy(block_inverse.at[0], inverse, load_sem.at[1]),
        pltpu.make_async_copy(coupling_left.at[0], left, load_sem.at[2]),
        pltpu.make_async_copy(coupling_right, right, load_sem.at[3]),
    ]
    near_loads = [
        pltpu.make_async_copy(columns_hbm, near_columns, load_sem.at[4]),
        pltpu.make_async_copy(rank_hbm, pair_rank, load_sem.at[5]),
        pltpu.make_async_copy(right_side.at[0], side, load_sem.at[6]),
        pltpu.make_async_copy(near_values.at[0], values, load_sem.at[7]),
    ]
    for copy in bases + near_loads + [own]:
        copy.start()

    pl.semaphore_wait(barrier, panels - 1 + ships - 1)
    spread = to_panels(0, lambda step: current.at[0], lambda step: ring.at[panel])
    for copy in spread:
        copy.start()

    for copy in bases:
        copy.wait()
    partners = [plan[k, ship] for k in range(rounds)]
    inv = [inverse[b].reshape(2 * block, block) for b in range(blocks)]
    raw = [left[p] for p in partners]
    moved = []
    for b in range(blocks):
        rows = jnp.concatenate(
            [r[y, :, b * block : (b + 1) * block] for y in range(2) for r in raw], axis=0
        )
        moved.append(complex_pair(dot_nt(rows, inv[b]), rounds * rank, block))
    moved_re = jnp.concatenate([m[0] for m in moved], axis=1)
    moved_im = jnp.concatenate([m[1] for m in moved], axis=1)
    spreaders = []
    for k in range(rounds):
        cut = slice(k * rank, (k + 1) * rank)
        spreaders.append(times_i(moved_re[cut], moved_im[cut]).astype(BF16))
    gatherers = []
    for p in partners:
        re, im = right[p, 0, 0], right[p, 0, 1]
        gatherers.append(
            jnp.concatenate(
                [jnp.concatenate([re, -im], axis=1), jnp.concatenate([im, re], axis=1)], axis=0
            )
        )
    share = rank // panels
    for index, (k, j) in enumerate(pairs):
        link = dot_nt(spreaders[j][:rank], gatherers[k]).astype(BF16)
        for target in range(panels):
            link_out[target, index] = link[target * share : (target + 1) * share]
    scatter = to_panels(
        1, lambda step: link_out.at[(panel + step) % panels], lambda step: link_in.at[step - 1]
    )
    for copy in scatter:
        copy.start()

    for copy in near_loads + [own]:
        copy.wait()
    for copy in spread:
        copy.wait_recv()

    def source_block(column):
        held = ring[column // blocks].reshape(2 * rhs, blocks * block)
        chosen = held[:, :block]
        for b in range(1, blocks):
            chosen = jnp.where(column % blocks == b, held[:, b * block : (b + 1) * block], chosen)
        return chosen

    start_re, start_im = [], []
    for b in range(blocks):
        picked = jnp.concatenate([source_block(near_columns[0, b, n]) for n in range(terms)], axis=1)
        weights = jnp.concatenate(
            [values[b, n].reshape(2 * block, block) for n in range(terms)], axis=1
        )
        re, im = complex_pair(dot_nt(picked, weights), rhs, block)
        cols = slice(b * block, (b + 1) * block)
        rest = jnp.concatenate([side[0, :, cols] - re, side[1, :, cols] - im], axis=0)
        re, im = complex_pair(dot_nt(rest.astype(BF16), inv[b]), rhs, block)
        start_re.append(re)
        start_im.append(im)
    total = jnp.concatenate(start_re + start_im, axis=1)
    sent = total.astype(BF16)
    own_parts = [dot_nt(sent, g) for g in gatherers]
    for k in range(rounds):
        part_out[k] = own_parts[k].astype(BF16)
    part_flight = to_panels(2, lambda step: part_out, lambda step: part_in.at[step - 1])
    for copy in part_flight:
        copy.start()

    for copy in scatter:
        copy.wait_recv()
    for index in range(len(pairs)):
        summed = link_out[panel, index].astype(F32)
        for step in range(1, panels):
            summed = summed + link_in[step - 1, index].astype(F32)
        all_links[ship, panel, index] = summed.astype(BF16)
    piece = all_links.at[ship, panel]
    link_flight = to_panels(3, lambda step: piece, lambda step: piece)
    for copy in link_flight:
        copy.start()

    for copy in part_flight:
        copy.wait_recv()
    for k in range(rounds):
        summed = own_parts[k]
        for step in range(1, panels):
            summed = summed + part_in[step - 1, k].astype(F32)
        all_parts[ship, k] = summed.astype(BF16)
    part_ships = to_ships(0, all_parts.at[ship])
    for copy in part_ships:
        copy.start()
    for copy in link_flight:
        copy.wait_recv()
    link_ships = to_ships(1, all_links.at[ship])
    for copy in link_ships:
        copy.start()
    for copy in part_ships + link_ships:
        copy.wait_recv()

    lane = lax.broadcasted_iota(jnp.int32, (rhs, 2 * rank), 1)
    lane = jnp.where(lane < rank, lane, lane - rank)

    def received(k, target, partner):
        value = all_parts[partner, k].astype(F32)
        for j in range(k):
            index = pairs.index((k, j))
            rows = jnp.concatenate(
                [all_links[partner, q, index] for q in range(panels)], axis=0
            ).astype(F32)
            link = times_i(rows[:, :rank], rows[:, rank:]).astype(BF16)
            value = value - dot_nn(received(j, partner, plan[j, partner]), link)
        return jnp.where(lane < pair_rank[target, partner], value, 0.0).astype(BF16)

    for k in range(rounds):
        total = total - dot_nn(received(k, ship, partners[k]), spreaders[k])
    width = blocks * block
    field[0, 0] = total[:, :width]
    field[0, 1] = total[:, width:]
    for copy in spread + scatter + part_flight + link_flight + part_ships + link_ships:
        copy.wait_send()


def few_ships(ships, panels, right_side, current, near_values, near_columns, block_inverse, coupling_right, coupling_left, pair_rank, plan):
    blocks = near_values.shape[1]
    block = near_values.shape[-1]
    rhs = current.shape[2]
    rank = coupling_left.shape[3]
    rounds = plan.shape[0]
    links = rounds * (rounds - 1) // 2
    share = rank // panels
    anywhere = pl.BlockSpec(memory_space=pl.ANY)
    return pl.pallas_call(
        functools.partial(sweep_kernel, ships, panels),
        out_shape=pltpu.VMEM(right_side.shape, F32),
        in_specs=[anywhere] * 9,
        out_specs=pl.BlockSpec(memory_space=pltpu.VMEM),
        scratch_shapes=[
            pltpu.SMEM(near_columns.shape, jnp.int32),
            pltpu.SMEM(pair_rank.shape, jnp.int32),
            pltpu.SMEM(plan.shape, jnp.int32),
            pltpu.VMEM((panels, 2, rhs, blocks * block), BF16),
            pltpu.VMEM(right_side.shape[1:], F32),
            pltpu.VMEM(near_values.shape[1:], BF16),
            pltpu.VMEM(block_inverse.shape[1:], BF16),
            pltpu.VMEM(coupling_right.shape, BF16),
            pltpu.VMEM(coupling_left.shape[1:], BF16),
            pltpu.VMEM((panels, links, share, 2 * rank), BF16),
            pltpu.VMEM((panels - 1, links, share, 2 * rank), BF16),
            pltpu.VMEM((ships, panels, links, share, 2 * rank), BF16),
            pltpu.VMEM((rounds, rhs, 2 * rank), BF16),
            pltpu.VMEM((panels - 1, rounds, rhs, 2 * rank), BF16),
            pltpu.VMEM((ships, rounds, rhs, 2 * rank), BF16),
            pltpu.SemaphoreType.DMA((9,)),
            pltpu.SemaphoreType.DMA((4, panels - 1)),
            pltpu.SemaphoreType.DMA((4, panels - 1)),
            pltpu.SemaphoreType.DMA((2, ships - 1)),
            pltpu.SemaphoreType.DMA((2, ships - 1)),
        ],
        compiler_params=pltpu.CompilerParams(
            collective_id=0,
            has_side_effects=True,
            vmem_limit_bytes=60 * 1024 * 1024,
        ),
    )(
        near_columns,
        pair_rank,
        plan,
        right_side,
        current,
        near_values,
        block_inverse,
        coupling_right,
        coupling_left,
    )


def pair_up(product, rhs_count):
    real_src = product[:, :rhs_count]
    imag_src = product[:, rhs_count:]
    return jnp.stack([real_src[0] - imag_src[1], imag_src[0] + real_src[1]])


def near_field(values, columns, gathered):
    rhs_count = gathered.shape[1]
    block_len = values.shape[-1]
    cell_rows = gathered.reshape(2 * rhs_count, -1, block_len)
    picked = jnp.stack(
        [
            jnp.stack(
                [
                    lax.dynamic_index_in_dim(cell_rows, columns[i, n], 1, keepdims=False)
                    for n in range(columns.shape[1])
                ],
                axis=1,
            )
            for i in range(columns.shape[0])
        ],
        axis=1,
    )
    product = jnp.einsum("cinu,inztu->zcit", picked, values, preferred_element_type=jnp.float32)
    return pair_up(product, rhs_count).reshape(2, rhs_count, -1)


def apply_inverse(inverse, rest):
    rhs_count = rest.shape[1]
    block_len = inverse.shape[-1]
    rounded = rest.astype(jnp.bfloat16).reshape(2 * rhs_count, -1, block_len)
    product = jnp.einsum("ciu,iztu->zcit", rounded, inverse, preferred_element_type=jnp.float32)
    return pair_up(product, rhs_count).reshape(2, rhs_count, -1)


def compress(right_basis, sent):
    rhs_count = sent.shape[1]
    flat = sent.reshape(2 * rhs_count, -1)
    grams = jnp.einsum("zan,cn->zac", right_basis, flat, preferred_element_type=jnp.float32)
    return jnp.stack(
        [
            grams[0, :, :rhs_count] - grams[1, :, rhs_count:],
            grams[0, :, rhs_count:] + grams[1, :, :rhs_count],
        ]
    )


def expand(received, left_basis):
    outer = jnp.einsum("yac,zan->yzcn", received, left_basis, preferred_element_type=jnp.float32)
    return jnp.stack([outer[0, 0] - outer[1, 1], outer[0, 1] + outer[1, 0]])


def any_ships(
    right_side,
    current,
    near_values,
    near_columns,
    block_inverse,
    coupling_right,
    coupling_left,
    pair_rank,
    plan,
):
    gathered = lax.all_gather(current[0], "panel", axis=2, tiled=True)
    rest = right_side[0] - near_field(near_values[0], near_columns[0], gathered)
    iterate = apply_inverse(block_inverse[0], rest)
    own_ship = lax.axis_index("ship")
    ship_count = coupling_left.shape[1]
    rank_index = lax.iota(jnp.int32, coupling_left.shape[3])
    for round_index in range(plan.shape[0]):
        partner = plan[round_index, own_ship]
        right_basis = lax.dynamic_index_in_dim(coupling_right, partner, 0, keepdims=False)[0]
        partial_value = compress(right_basis, iterate.astype(jnp.bfloat16))
        slot_mask = (lax.iota(jnp.int32, ship_count) == partner).astype(jnp.float32)
        spread = slot_mask[:, None, None, None] * partial_value[None]
        summed = lax.psum(spread, ("ship", "panel"))
        incoming = lax.dynamic_index_in_dim(summed, own_ship, 0, keepdims=False)
        keep_mask = rank_index < pair_rank[own_ship, partner]
        received = jnp.where(keep_mask[None, :, None], incoming, jnp.float32(0.0)).astype(
            jnp.bfloat16
        )
        left_basis = lax.dynamic_index_in_dim(coupling_left[0], partner, 0, keepdims=False)
        rest = rest - expand(received, left_basis)
        iterate = apply_inverse(block_inverse[0], rest)
    return iterate[None]


def solution(mesh):
    placed = (
        P(("parts", "ship"), None, None, "panel"),
        P(("parts", "ship"), None, None, "panel"),
        P(("parts", "ship"), "panel", None, None, None, None),
        P(("parts", "ship"), "panel", None),
        P(("parts", "ship"), "panel", None, None, None),
        P("parts", "ship", None, None, "panel"),
        P(("parts", "ship"), None, None, None, "panel"),
        P(),
        P(),
    )
    ships, panels = mesh.shape["ship"], mesh.shape["panel"]
    on_device = functools.partial(few_ships, ships, panels) if ships == 4 and panels == 4 else any_ships
    return jax.shard_map(
        on_device,
        mesh=mesh,
        in_specs=placed,
        out_specs=P(("parts", "ship"), None, None, "panel"),
        check_vma=False,
    )
```
